32 devices in a mesh: groups: 2 (over y), dp: 4 (over z), tensor: 2 (over x), seq: 2 (over core).
Axes of the slice: x: 2, y: 2, z: 4, core: 2. Of those that a mesh axis runs over, the one named last changes fastest.
Arguments:
- pas_q: bfloat16 [32, 256, 1024], P(('groups', 'dp', 'seq'), None, 'tensor'), parts along dimension 0, may hold values from -12 to 12
- pas_kv: bfloat16 [2, 32, 256, 256], P(None, ('groups', 'dp', 'seq'), None, 'tensor'), parts along dimension 1, may hold values from -6 to 6
- pre_kv: bfloat16 [2, 8, 256, 256], P(None, ('groups', 'dp'), 'seq', 'tensor'), parts along dimension 1, may hold values from -8 to 8
- d_out: bfloat16 [32, 256, 1024], P(('groups', 'dp', 'seq'), None, 'tensor'), parts along dimension 0, may hold values from -24 to 24
- passage_query: int32 [32], P('groups'), parts along dimension 0, may hold values from 0 to 3, never falling along the last dimension, each value on 1 to 8 neighbouring positions
- query_owner: int32 [8], P('groups'), parts along dimension 0, may hold values from 0 to 3, each once
Outputs:
- attn_out: bfloat16 [32, 256, 1024], P(('groups', 'dp', 'seq'), None, 'tensor'), parts along dimension 0
- d_q: bfloat16 [32, 256, 1024], P(('groups', 'dp', 'seq'), None, 'tensor'), parts along dimension 0
- d_pas_kv: bfloat16 [2, 32, 256, 256], P(None, ('groups', 'dp', 'seq'), None, 'tensor'), parts along dimension 1
- d_pre_kv: bfloat16 [2, 8, 256, 256], P(None, ('groups', 'dp'), 'seq', 'tensor'), parts along dimension 1
The draws below stay inside these ranges and needn't reach their ends.
There are 2 independent parts, one for each index of `groups`. The reference program is written for one: setup_inputs(seed, part) draws one part's arguments, and reference() takes and returns one part's arrays. A program takes and returns all parts, laid end to end along the dimension named above; each array names one. Nothing has to cross between parts.
Inputs may be any that keep to these rules, and one draw needn't show every extreme that they name: `passage_query`: passages are packed by query: the candidates of one query are consecutive passages; every query has 1 to 8 candidates and one query has exactly 8. `query_owner`: each slot holds the prefix of exactly one query.
All inputs are finite; a program needn't handle non-finite values.
Results may differ from the reference program's by a relative error of at most 0.02.
Values may be sent and summed in bfloat16 or wider, within the bound.
A program may use at most 64 MiB of HBM per device.

```python
import math
import jax
import jax.numpy as jnp
import numpy as np
from jax import lax

HD = 128
GROUP = 4
PRE = 256
PAS = 256
P_DEV = 4
KV_HEADS = 2
Q_HEADS = 8
QUERIES = 4
PASSAGES = 16
CAND_MOST = 8
N_SEQ = 2


def draw_pas_q(key, part):
    key = jax.random.fold_in(key, 11)
    full_shape = (PASSAGES, PAS, Q_HEADS, HD)
    drawn = jnp.clip(2.0 * jax.random.normal(key, full_shape, jnp.float32), -12.0, 12.0)
    return drawn.reshape(PASSAGES, PAS, Q_HEADS * HD).astype(jnp.bfloat16)


def draw_pre_kv(key, part):
    key = jax.random.fold_in(key, 23)
    full_shape = (2, QUERIES, PRE, KV_HEADS, HD)
    drawn = jnp.clip(jax.random.normal(key, full_shape, jnp.float32), -6.0, 6.0)
    return drawn.reshape(2, QUERIES, PRE, KV_HEADS * HD).astype(jnp.bfloat16)


def levels(stream_key, extent, split, smallest, high):
    loudness = 1.0
    for axis_at, parts in split:
        steps = jax.random.uniform(jax.random.fold_in(jax.random.fold_in(stream_key, 6), axis_at), (parts,), jnp.float32, smallest / len(split), high / len(split))
        loudness = loudness * jnp.repeat(jnp.exp(steps), extent[axis_at] // parts).reshape((-1,) + (1,) * (len(extent) - 1 - axis_at))
    return loudness


def split_up(number_of, total, reach, lean):
    weights = [(1 << 20) // math.isqrt(grade ** lean) + 1 for grade in range(2, number_of + 1)]
    rest, holding = total - reach - (number_of - 1), [1] * (number_of - 1)
    while rest > 0:
        movable = [i for i in range(number_of - 1) if holding[i] < reach]
        mass, budget = sum([weights[i] for i in movable]), rest
        for i in movable:
            extra = min(reach - holding[i], max(1, budget * weights[i] // mass), rest)
            holding[i] = holding[i] + extra
            rest = rest - extra
    return np.array([reach] + holding)


def ragged(key, number_of, total, bound, lean):
    if number_of == 2:
        one = jax.random.randint(key, (), max(1, total - bound), min(bound, total - 1) + 1)
        return jnp.stack([one, total - one])
    lengths = jnp.asarray(split_up(number_of, total, bound, lean), jnp.int32)
    couples = (number_of - 1) // 2
    donor, receiver = lengths[1:1 + 2 * couples:2], lengths[2:2 + 2 * couples:2]
    slack = jnp.minimum(donor - 1, bound - receiver)
    passed = jax.random.randint(jax.random.fold_in(key, 1), (couples,), 0, 1 << 20) % (slack + 1)
    lengths = lengths.at[1:1 + 2 * couples:2].set(donor - passed).at[2:2 + 2 * couples:2].set(receiver + passed)
    return lengths[jax.random.permutation(jax.random.fold_in(key, 2), number_of)]


def gaussian(stream_key, extent, spread, limit, cuts=(), kind=jnp.bfloat16):
    factor_of = levels(stream_key, extent, cuts, -0.22, 0.18) if cuts else 1.0
    result = jax.random.normal(stream_key, extent, jnp.float32) * spread * factor_of
    return jnp.minimum(jnp.maximum(result, -limit), limit).astype(kind)


def setup_inputs(seed: int = 0, part: int = 0) -> dict:
    key_of = jax.random.split(jax.random.key(seed), 7)
    part_splits = jax.random.split(jax.random.fold_in(key_of[6], part), 7)
    pas_q = draw_pas_q(jax.random.fold_in(jax.random.fold_in(key_of[6], part), 71), part)
    pas_kv = gaussian(part_splits[1], (2, PASSAGES, PAS, KV_HEADS * HD), 1.0, 6.0, ((1, 8), (3, 2)))
    pre_kv = draw_pre_kv(jax.random.fold_in(jax.random.fold_in(key_of[6], part), 71), part)
    d_out = gaussian(part_splits[3], (PASSAGES, PAS, Q_HEADS * HD), 4.0, 24.0, ((0, 8), (2, 2)))
    passage_query = jnp.searchsorted(jnp.cumsum(ragged(part_splits[4], QUERIES, PASSAGES, CAND_MOST, 2)), jnp.arange(PASSAGES), side="right").astype(jnp.int32)
    query_owner = jax.random.permutation(part_splits[5], QUERIES).astype(jnp.int32)
    return dict(pas_q=pas_q, pas_kv=pas_kv, pre_kv=pre_kv, d_out=d_out, passage_query=passage_query, query_owner=query_owner)


def rounded(value):
    return lax.optimization_barrier(value.astype(jnp.bfloat16)).astype(jnp.float32)


def passage_pass(query_rows, passage_kv, prefix_kv, grad_rows):
    scaling = HD ** -0.5
    key_rows = jnp.concatenate([prefix_kv[0], passage_kv[0]], axis=0).astype(jnp.float32)
    value_rows = jnp.concatenate([prefix_kv[1], passage_kv[1]], axis=0).astype(jnp.float32)
    query_full = query_rows.astype(jnp.float32)
    grad_full = grad_rows.astype(jnp.float32)
    scores = jnp.einsum('tgrd,kgd->tgrk', query_full, key_rows) * scaling
    token_pos = jnp.arange(PAS)[:, None]
    key_pos = jnp.arange(PRE + PAS)[None, :] - PRE
    visible = key_pos <= token_pos
    scores = jnp.where(visible[:, None, None, :], scores, -jnp.inf)
    row_top = jnp.max(scores, axis=-1, keepdims=True)
    log_total = row_top + jnp.log(jnp.sum(jnp.exp(scores - row_top), axis=-1, keepdims=True))
    weights = jnp.exp(scores - log_total)
    weight_round = rounded(weights)
    out_round = rounded(jnp.einsum('tgrk,kgd->tgrd', weight_round, value_rows))
    row_delta = jnp.sum(grad_full * out_round, axis=-1, keepdims=True)
    prob_grad = jnp.einsum('tgrd,kgd->tgrk', grad_full, value_rows)
    score_grad = rounded(weights * (prob_grad - row_delta))
    query_grad = jnp.einsum('tgrk,kgd->tgrd', score_grad, key_rows) * scaling
    key_grad = jnp.einsum('tgrk,tgrd->kgd', score_grad, query_full) * scaling
    value_grad = jnp.einsum('tgrk,tgrd->kgd', weight_round, grad_full)
    grad_pair = jnp.stack([key_grad, value_grad], axis=0)
    passage_part = grad_pair[:, PRE:]
    prefix_part = grad_pair[:, :PRE]
    return out_round, query_grad, passage_part, prefix_part


def reference(pas_q, pas_kv, pre_kv, d_out, passage_query, query_owner):
    slot_ids = jnp.take(query_owner, passage_query).astype(jnp.int32)
    block_len = P_DEV // N_SEQ
    block_total = PASSAGES // block_len

    def one_passage(position):
        query_rows = lax.dynamic_index_in_dim(pas_q, position, 0, False).reshape(PAS, KV_HEADS, GROUP, HD)
        grad_rows = lax.dynamic_index_in_dim(d_out, position, 0, False).reshape(PAS, KV_HEADS, GROUP, HD)
        passage_kv = lax.dynamic_index_in_dim(pas_kv, position, 1, False).reshape(2, PAS, KV_HEADS, HD)
        slot_id = lax.dynamic_index_in_dim(slot_ids, position, 0, False)
        prefix_kv = lax.dynamic_index_in_dim(pre_kv, slot_id, 1, False).reshape(2, PRE, KV_HEADS, HD)
        return passage_pass(query_rows, passage_kv, prefix_kv, grad_rows)

    def one_block(grad_sum, block_id):
        first_row = (block_id * block_len).astype(jnp.int32)
        positions = first_row + jnp.arange(block_len, dtype=jnp.int32)
        out_round, query_grad, passage_part, prefix_part = lax.map(one_passage, positions)
        block_slots = lax.dynamic_slice_in_dim(slot_ids, first_row, block_len)
        selector = (block_slots[:, None] == jnp.arange(QUERIES, dtype=jnp.int32)[None, :]).astype(jnp.float32)
        partial_value = jnp.einsum('pq,pxkgd->xqkgd', selector, prefix_part, precision=lax.Precision.HIGHEST)
        grad_sum = grad_sum + rounded(partial_value)
        return grad_sum, (out_round.astype(jnp.bfloat16), query_grad.astype(jnp.bfloat16), passage_part.astype(jnp.bfloat16))

    initial = jnp.zeros((2, QUERIES, PRE, KV_HEADS, HD), jnp.float32)
    grad_sum, (out_rows, query_grads, pass_grads) = lax.scan(one_block, initial, jnp.arange(block_total, dtype=jnp.int32))
    attn_out = out_rows.reshape(PASSAGES, PAS, Q_HEADS * HD)
    d_q = query_grads.reshape(PASSAGES, PAS, Q_HEADS * HD)
    d_pas_kv = jnp.moveaxis(pass_grads.reshape(PASSAGES, 2, PAS, KV_HEADS * HD), 1, 0)
    d_pre_kv = grad_sum.reshape(2, QUERIES, PRE, KV_HEADS * HD).astype(jnp.bfloat16)
    return attn_out, d_q, d_pas_kv, d_pre_kv
```

```python
import math

import jax
import jax.numpy as jnp
from jax import lax
from jax.experimental import pallas as pl
from jax.experimental.pallas import tpu as pltpu
from jax.sharding import PartitionSpec as P

HD = 128
SCALE = HD ** (-0.5)
EXP_SCALE = SCALE * math.log2(math.e)
MASKED = -1e30
BF = jnp.bfloat16
F32 = jnp.float32


def dot(a, b):
    return jnp.dot(a, b, preferred_element_type=F32)


def make_kernel(n, count, heads, tokens, part):
    prefix = 2 * part

    def kernel(
        pq_ref, qo_ref, q_hbm, kv_hbm, pre_hbm, do_hbm,
        out_hbm, dq_hbm, dkv_hbm, dpre_hbm,
        q, do, kv, q_t, do_t, kv_t, e_own, dp_own, o_own, ds_pre, o_t, stat,
        pre, kv_pre, kv_pre_t, grad, own_grad, out, dq, dkv, dpre,
        send1, recv1, send2, recv2,
        load_sem, store_sem, own_sem,
        zs_sem, zr_sem, fs_sem, fr_sem, s1_sem, r1_sem, s2_sem, r2_sem,
    ):
        z = lax.axis_index("dp")
        c = lax.axis_index("seq")
        other = 1 - c

        loads = [
            pltpu.make_async_copy(q_hbm, q, load_sem.at[0]),
            pltpu.make_async_copy(kv_hbm, kv, load_sem.at[1]),
            pltpu.make_async_copy(do_hbm, do, load_sem.at[2]),
        ]
        for copy in loads:
            copy.start()
        own = pltpu.make_async_copy(pre_hbm.at[:, 0], pre.at[z, :, c], own_sem)
        own.start()

        barrier = pltpu.get_barrier_semaphore()
        for d in range(1, n):
            pl.semaphore_signal(barrier, inc=1, device_id={"dp": lax.rem(z + d, n)})
        pl.semaphore_signal(barrier, inc=1, device_id={"seq": other})
        pl.semaphore_wait(barrier, n)

        gathers = {}
        for d in range(1, n):
            gathers[d] = pltpu.make_async_remote_copy(
                src_ref=pre_hbm.at[:, 0], dst_ref=pre.at[z, :, c],
                send_sem=zs_sem.at[d], recv_sem=zr_sem.at[d],
                device_id={"dp": lax.rem(z + d, n)},
            )
            gathers[d].start()
        forwards = {}
        forwards[0] = pltpu.make_async_remote_copy(
            src_ref=pre_hbm.at[:, 0], dst_ref=pre.at[z, :, c],
            send_sem=fs_sem.at[0], recv_sem=fr_sem.at[0], device_id={"seq": other},
        )
        forwards[0].start()
        for copy in loads:
            copy.wait()

        for p in range(count):
            kv_t[0, p] = kv[0, p].T
            kv_t[1, p] = kv[1, p].T
        key_at = lax.broadcasted_iota(jnp.int32, (tokens, tokens), 0)
        token_at = lax.broadcasted_iota(jnp.int32, (tokens, tokens), 1)

        def own_part(h, _):
            cols = pl.ds(pl.multiple_of(h * HD, HD), HD)
            for p in range(count):
                qt = q[p, :, cols].T
                dt = do[p, :, cols].T
                q_t[p, h] = qt
                do_t[p, h] = dt
                scores = jnp.where(key_at <= token_at, dot(kv[0, p], qt), MASKED)
                top = jnp.max(scores, axis=0, keepdims=True)
                e = jnp.exp2((scores - top) * EXP_SCALE)
                stat[p, h, 0:1, :] = top
                stat[p, h, 1:2, :] = jnp.sum(e, axis=0, keepdims=True)
                e_own[p, h] = e
                o_own[p, h] = dot(kv_t[1, p], e.astype(BF))
                dp_own[p, h] = dot(kv[1, p], dt)
            return 0

        lax.fori_loop(0, heads, own_part, 0)

        own.wait()
        for d in range(1, n):
            gathers[d].wait_recv()
            source = lax.rem(z + n - d, n)
            forwards[d] = pltpu.make_async_remote_copy(
                src_ref=pre.at[source, :, c], dst_ref=pre.at[source, :, c],
                send_sem=fs_sem.at[d], recv_sem=fr_sem.at[d], device_id={"seq": other},
            )
            forwards[d].start()
        for d in range(n):
            forwards[d].wait_recv()

        first = (z * 2 + c) * count
        slots = [qo_ref[pq_ref[first + p]] for p in range(count)]
        for p in range(count):
            for x in range(2):
                rows = pre[slots[p], x].reshape(prefix, HD)
                kv_pre[x, p] = rows
                kv_pre_t[x, p] = rows.T
        grad[...] = jnp.zeros_like(grad)

        def prefix_part(h, _):
            cols = pl.ds(pl.multiple_of(h * HD, HD), HD)
            for p in range(count):
                dt = do_t[p, h]
                scores = dot(kv_pre[0, p], q_t[p, h])
                top_own = stat[p, h, 0:1, :]
                top = jnp.maximum(top_own, jnp.max(scores, axis=0, keepdims=True))
                shrink = jnp.exp2((top_own - top) * EXP_SCALE)
                e = jnp.exp2((scores - top) * EXP_SCALE)
                total = stat[p, h, 1:2, :] * shrink + jnp.sum(e, axis=0, keepdims=True)
                inverse = 1.0 / total
                w = e * inverse
                wb = w.astype(BF)
                factor = shrink * inverse
                o = (o_own[p, h] * factor + dot(kv_pre_t[1, p], wb)).astype(BF)
                o_t[p, h] = o
                delta = jnp.sum(dt.astype(F32) * o.astype(F32), axis=0, keepdims=True)
                stat[p, h, 2:3, :] = factor
                stat[p, h, 3:4, :] = delta
                ds = (w * (dot(kv_pre[1, p], dt) - delta)).astype(BF)
                ds_pre[p, h] = ds
                grad[p, 0] += dot(ds, q[p, :, cols])
                grad[p, 1] += dot(wb, do[p, :, cols])
            return 0

        lax.fori_loop(0, heads, prefix_part, 0)

        def half_terms(d, half):
            slot = lax.rem(z + d, n)
            rows = pl.ds(pl.multiple_of(half * part, part), part)
            values = []
            for x in range(2):
                value = None
                for p in range(count):
                    use = jnp.where(slots[p] == slot, SCALE if x == 0 else 1.0, 0.0).astype(F32)
                    term = grad[p, x, rows, :] * use
                    value = term if value is None else value + term
                values.append(value)
            return values

        order = list(range(1, n)) + [0]
        pairs = {}
        for d in order:
            values = half_terms(d, other)
            for x in range(2):
                send1[d, x] = values[x].astype(BF)
            pairs[d] = pltpu.make_async_remote_copy(
                src_ref=send1.at[d], dst_ref=recv1.at[d],
                send_sem=s1_sem.at[d], recv_sem=r1_sem.at[d], device_id={"seq": other},
            )
            pairs[d].start()

        for p in range(count):
            for h in range(heads):
                out[p, :, h * HD:(h + 1) * HD] = o_t[p, h].T
        store_out = pltpu.make_async_copy(out, out_hbm, store_sem.at[0])
        store_out.start()

        spreads = {}
        for d in range(1, n):
            values = half_terms(d, c)
            pairs[d].wait_recv()
            for x in range(2):
                send2[d, x] = (values[x] + recv1[d, x].astype(F32)).astype(BF)
            spreads[d] = pltpu.make_async_remote_copy(
                src_ref=send2.at[d], dst_ref=recv2.at[d],
                send_sem=s2_sem.at[d], recv_sem=r2_sem.at[d],
                device_id={"dp": lax.rem(z + d, n)},
            )
            spreads[d].start()

        def rest_part(h, carry):
            cols = pl.ds(pl.multiple_of(h * HD, HD), HD)
            for p in range(count):
                w = e_own[p, h] * stat[p, h, 2:3, :]
                ds = (w * (dp_own[p, h] - stat[p, h, 3:4, :])).astype(BF)
                own_grad[p, 0] += dot(ds, q[p, :, cols])
                own_grad[p, 1] += dot(w.astype(BF), do[p, :, cols])
                back = dot(kv_t[0, p], ds) + dot(kv_pre_t[0, p], ds_pre[p, h])
                dq[p, :, cols] = (back * SCALE).astype(BF).T
            return carry

        own_grad[...] = jnp.zeros_like(own_grad)
        lax.fori_loop(0, heads, rest_part, 0)
        store_dq = pltpu.make_async_copy(dq, dq_hbm, store_sem.at[1])
        store_dq.start()
        for p in range(count):
            dkv[0, p] = (own_grad[p, 0] * SCALE).astype(BF)
            dkv[1, p] = own_grad[p, 1].astype(BF)
        store_dkv = pltpu.make_async_copy(dkv, dkv_hbm, store_sem.at[2])
        store_dkv.start()

        values = half_terms(0, c)
        pairs[0].wait_recv()
        totals = [values[x] + recv1[0, x].astype(F32) for x in range(2)]
        for d in range(1, n):
            spreads[d].wait_recv()
            for x in range(2):
                totals[x] = totals[x] + recv2[d, x].astype(F32)
        for x in range(2):
            dpre[x, 0] = totals[x].astype(BF)
        store_dpre = pltpu.make_async_copy(dpre, dpre_hbm, store_sem.at[3])
        store_dpre.start()

        for d in range(1, n):
            gathers[d].wait_send()
            spreads[d].wait_send()
        for d in range(n):
            forwards[d].wait_send()
            pairs[d].wait_send()
        store_out.wait()
        store_dq.wait()
        store_dkv.wait()
        store_dpre.wait()

    return kernel


def on_device(n, pas_q, pas_kv, pre_kv, d_out, passage_query, query_owner):
    count, tokens, width = pas_q.shape
    heads = width // HD
    part = pre_kv.shape[2]
    prefix = 2 * part
    assert pre_kv.shape[1] == 1
    block = (2, part, HD)
    any_spec = pl.BlockSpec(memory_space=pl.ANY)
    smem_spec = pl.BlockSpec(memory_space=pltpu.SMEM)
    square = (count, heads, tokens, tokens)
    dma = pltpu.SemaphoreType.DMA
    call = pl.pallas_call(
        make_kernel(n, count, heads, tokens, part),
        out_shape=(
            jax.ShapeDtypeStruct(pas_q.shape, BF),
            jax.ShapeDtypeStruct(pas_q.shape, BF),
            jax.ShapeDtypeStruct(pas_kv.shape, BF),
            jax.ShapeDtypeStruct(pre_kv.shape, BF),
        ),
        in_specs=[smem_spec, smem_spec, any_spec, any_spec, any_spec, any_spec],
        out_specs=(any_spec,) * 4,
        scratch_shapes=[
            pltpu.VMEM(pas_q.shape, BF),
            pltpu.VMEM(pas_q.shape, BF),
            pltpu.VMEM(pas_kv.shape, BF),
            pltpu.VMEM((count, heads, HD, tokens), BF),
            pltpu.VMEM((count, heads, HD, tokens), BF),
            pltpu.VMEM((2, count, HD, tokens), BF),
            pltpu.VMEM(square, F32),
            pltpu.VMEM(square, F32),
            pltpu.VMEM((count, heads, HD, tokens), F32),
            pltpu.VMEM((count, heads, prefix, tokens), BF),
            pltpu.VMEM((count, heads, HD, tokens), BF),
            pltpu.VMEM((count, heads, 8, tokens), F32),
            pltpu.VMEM((n, 2, 2, part, HD), BF),
            pltpu.VMEM((2, count, prefix, HD), BF),
            pltpu.VMEM((2, count, HD, prefix), BF),
            pltpu.VMEM((count, 2, prefix, HD), F32),
            pltpu.VMEM((count, 2, tokens, HD), F32),
            pltpu.VMEM(pas_q.shape, BF),
            pltpu.VMEM(pas_q.shape, BF),
            pltpu.VMEM(pas_kv.shape, BF),
            pltpu.VMEM(pre_kv.shape, BF),
            pltpu.VMEM((n,) + block, BF),
            pltpu.VMEM((n,) + block, BF),
            pltpu.VMEM((n,) + block, BF),
            pltpu.VMEM((n,) + block, BF),
            dma((3,)),
            dma((4,)),
            dma,
        ] + [dma((n,))] * 8,
        compiler_params=pltpu.CompilerParams(
            collective_id=0, has_side_effects=True, vmem_limit_bytes=40 * 1024 * 1024
        ),
    )
    return call(passage_query, query_owner, pas_q, pas_kv, pre_kv, d_out)


def solution(mesh):
    n = mesh.shape["dp"]

    def step(*arrays):
        return on_device(n, *arrays)

    return jax.shard_map(
        step,
        mesh=mesh,
        in_specs=(
            P(("groups", "dp", "seq"), None, "tensor"),
            P(None, ("groups", "dp", "seq"), None, "tensor"),
            P(None, ("groups", "dp"), "seq", "tensor"),
            P(("groups", "dp", "seq"), None, "tensor"),
            P("groups"),
            P("groups"),
        ),
        out_specs=(
            P(("groups", "dp", "seq"), None, "tensor"),
            P(("groups", "dp", "seq"), None, "tensor"),
            P(None, ("groups", "dp", "seq"), None, "tensor"),
            P(None, ("groups", "dp"), "seq", "tensor"),
        ),
        check_vma=False,
    )
```

```python
import math

import jax
import jax.numpy as jnp
from jax import lax
from jax.experimental import pallas as pl
from jax.experimental.pallas import tpu as pltpu
from jax.sharding import PartitionSpec as P

HD = 128
SCALE = HD ** (-0.5)
EXP_SCALE = SCALE * math.log2(math.e)
MASKED = -1e30
BF = jnp.bfloat16
F32 = jnp.float32


def dot(a, b):
    return jnp.dot(a, b, preferred_element_type=F32)


def make_kernel(n, count, heads, tokens, part):
    prefix = 2 * part

    def kernel(
        pq_hbm, qo_hbm, q_hbm, kv_hbm, pre_hbm, do_hbm,
        out_hbm, dq_hbm, dkv_hbm, dpre_hbm,
        q, do, kv, q_t, do_t, kv_t, e_own, dp_own, o_own, ds_pre, o_t, stat,
        pre, kv_pre, kv_pre_t, grad, own_grad, out, dq, dkv, dpre,
        send1, recv1, send2, recv2,
        pq_ref, qo_ref, load_sem, store_sem, own_sem,
        zs_sem, zr_sem, fs_sem, fr_sem, s1_sem, r1_sem, s2_sem, r2_sem,
    ):
        z = lax.axis_index("dp")
        c = lax.axis_index("seq")
        other = 1 - c

        loads = [
            pltpu.make_async_copy(q_hbm, q, load_sem.at[0]),
            pltpu.make_async_copy(kv_hbm, kv, load_sem.at[1]),
            pltpu.make_async_copy(do_hbm, do, load_sem.at[2]),
            pltpu.make_async_copy(pq_hbm, pq_ref, load_sem.at[3]),
            pltpu.make_async_copy(qo_hbm, qo_ref, load_sem.at[4]),
        ]
        for copy in loads:
            copy.start()
        own = pltpu.make_async_copy(pre_hbm.at[:, 0], pre.at[z, :, c], own_sem)
        own.start()

        barrier = pltpu.get_barrier_semaphore()
        for d in range(1, n):
            pl.semaphore_signal(barrier, inc=1, device_id={"dp": lax.rem(z + d, n)})
        pl.semaphore_signal(barrier, inc=1, device_id={"seq": other})
        pl.semaphore_wait(barrier, n)

        gathers = {}
        for d in range(1, n):
            gathers[d] = pltpu.make_async_remote_copy(
                src_ref=pre_hbm.at[:, 0], dst_ref=pre.at[z, :, c],
                send_sem=zs_sem.at[d], recv_sem=zr_sem.at[d],
                device_id={"dp": lax.rem(z + d, n)},
            )
            gathers[d].start()
        forwards = {}
        forwards[0] = pltpu.make_async_remote_copy(
            src_ref=pre_hbm.at[:, 0], dst_ref=pre.at[z, :, c],
            send_sem=fs_sem.at[0], recv_sem=fr_sem.at[0], device_id={"seq": other},
        )
        forwards[0].start()
        for copy in loads:
            copy.wait()

        for p in range(count):
            kv_t[0, p] = kv[0, p].T
            kv_t[1, p] = kv[1, p].T
        key_at = lax.broadcasted_iota(jnp.int32, (tokens, tokens), 0)
        token_at = lax.broadcasted_iota(jnp.int32, (tokens, tokens), 1)

        def own_part(h, _):
            cols = pl.ds(pl.multiple_of(h * HD, HD), HD)
            for p in range(count):
                qt = q[p, :, cols].T
                dt = do[p, :, cols].T
                q_t[p, h] = qt
                do_t[p, h] = dt
                scores = jnp.where(key_at <= token_at, dot(kv[0, p], qt), MASKED)
                top = jnp.max(scores, axis=0, keepdims=True)
                e = jnp.exp2((scores - top) * EXP_SCALE)
                stat[p, h, 0:1, :] = top
                stat[p, h, 1:2, :] = jnp.sum(e, axis=0, keepdims=True)
                e_own[p, h] = e
                o_own[p, h] = dot(kv_t[1, p], e.astype(BF))
                dp_own[p, h] = dot(kv[1, p], dt)
            return 0

        lax.fori_loop(0, heads, own_part, 0)

        own.wait()
        for d in range(1, n):
            gathers[d].wait_recv()
            source = lax.rem(z + n - d, n)
            forwards[d] = pltpu.make_async_remote_copy(
                src_ref=pre.at[source, :, c], dst_ref=pre.at[source, :, c],
                send_sem=fs_sem.at[d], recv_sem=fr_sem.at[d], device_id={"seq": other},
            )
            forwards[d].start()
        for d in range(n):
            forwards[d].wait_recv()

        first = (z * 2 + c) * count
        slots = [qo_ref[pq_ref[first + p]] for p in range(count)]
        for p in range(count):
            for x in range(2):
                rows = pre[slots[p], x].reshape(prefix, HD)
                kv_pre[x, p] = rows
                kv_pre_t[x, p] = rows.T
        grad[...] = jnp.zeros_like(grad)

        def prefix_part(h, _):
            cols = pl.ds(pl.multiple_of(h * HD, HD), HD)
            for p in range(count):
                dt = do_t[p, h]
                scores = dot(kv_pre[0, p], q_t[p, h])
                top_own = stat[p, h, 0:1, :]
                top = jnp.maximum(top_own, jnp.max(scores, axis=0, keepdims=True))
                shrink = jnp.exp2((top_own - top) * EXP_SCALE)
                e = jnp.exp2((scores - top) * EXP_SCALE)
                total = stat[p, h, 1:2, :] * shrink + jnp.sum(e, axis=0, keepdims=True)
                inverse = 1.0 / total
                w = e * inverse
                wb = w.astype(BF)
                factor = shrink * inverse
                o = (o_own[p, h] * factor + dot(kv_pre_t[1, p], wb)).astype(BF)
                o_t[p, h] = o
                delta = jnp.sum(dt.astype(F32) * o.astype(F32), axis=0, keepdims=True)
                stat[p, h, 2:3, :] = factor
                stat[p, h, 3:4, :] = delta
                ds = (w * (dot(kv_pre[1, p], dt) - delta)).astype(BF)
                ds_pre[p, h] = ds
                grad[p, 0] += dot(ds, q[p, :, cols])
                grad[p, 1] += dot(wb, do[p, :, cols])
            return 0

        lax.fori_loop(0, heads, prefix_part, 0)

        def half_terms(d, half):
            slot = lax.rem(z + d, n)
            rows = pl.ds(pl.multiple_of(half * part, part), part)
            values = []
            for x in range(2):
                value = None
                for p in range(count):
                    use = jnp.where(slots[p] == slot, SCALE if x == 0 else 1.0, 0.0).astype(F32)
                    term = grad[p, x, rows, :] * use
                    value = term if value is None else value + term
                values.append(value)
            return values

        order = list(range(1, n)) + [0]
        pairs = {}
        for d in order:
            values = half_terms(d, other)
            for x in range(2):
                send1[d, x] = values[x].astype(BF)
            pairs[d] = pltpu.make_async_remote_copy(
                src_ref=send1.at[d], dst_ref=recv1.at[d],
                send_sem=s1_sem.at[d], recv_sem=r1_sem.at[d], device_id={"seq": other},
            )
            pairs[d].start()

        for p in range(count):
            for h in range(heads):
                out[p, :, h * HD:(h + 1) * HD] = o_t[p, h].T
        store_out = pltpu.make_async_copy(out, out_hbm, store_sem.at[0])
        store_out.start()

        spreads = {}
        for d in range(1, n):
            values = half_terms(d, c)
            pairs[d].wait_recv()
            for x in range(2):
                send2[d, x] = (values[x] + recv1[d, x].astype(F32)).astype(BF)
            spreads[d] = pltpu.make_async_remote_copy(
                src_ref=send2.at[d], dst_ref=recv2.at[d],
                send_sem=s2_sem.at[d], recv_sem=r2_sem.at[d],
                device_id={"dp": lax.rem(z + d, n)},
            )
            spreads[d].start()

        def rest_part(h, carry):
            cols = pl.ds(pl.multiple_of(h * HD, HD), HD)
            for p in range(count):
                w = e_own[p, h] * stat[p, h, 2:3, :]
                ds = (w * (dp_own[p, h] - stat[p, h, 3:4, :])).astype(BF)
                own_grad[p, 0] += dot(ds, q[p, :, cols])
                own_grad[p, 1] += dot(w.astype(BF), do[p, :, cols])
                back = dot(kv_t[0, p], ds) + dot(kv_pre_t[0, p], ds_pre[p, h])
                dq[p, :, cols] = (back * SCALE).astype(BF).T
            return carry

        own_grad[...] = jnp.zeros_like(own_grad)
        lax.fori_loop(0, heads, rest_part, 0)
        store_dq = pltpu.make_async_copy(dq, dq_hbm, store_sem.at[1])
        store_dq.start()
        for p in range(count):
            dkv[0, p] = (own_grad[p, 0] * SCALE).astype(BF)
            dkv[1, p] = own_grad[p, 1].astype(BF)
        store_dkv = pltpu.make_async_copy(dkv, dkv_hbm, store_sem.at[2])
        store_dkv.start()

        values = half_terms(0, c)
        pairs[0].wait_recv()
        totals = [values[x] + recv1[0, x].astype(F32) for x in range(2)]
        for d in range(1, n):
            spreads[d].wait_recv()
            for x in range(2):
                totals[x] = totals[x] + recv2[d, x].astype(F32)
        for x in range(2):
            dpre[x, 0] = totals[x].astype(BF)
        store_dpre = pltpu.make_async_copy(dpre, dpre_hbm, store_sem.at[3])
        store_dpre.start()

        for d in range(1, n):
            gathers[d].wait_send()
            spreads[d].wait_send()
        for d in range(n):
            forwards[d].wait_send()
            pairs[d].wait_send()
        store_out.wait()
        store_dq.wait()
        store_dkv.wait()
        store_dpre.wait()

    return kernel

def store_kernel(*refs):
    sems = refs[-1]
    count = (len(refs) - 1) // 2
    copies = [
        pltpu.make_async_copy(refs[i], refs[count + i], sems.at[i]) for i in range(count)
    ]
    for copy in copies:
        copy.start()
    for copy in copies:
        copy.wait()


def store_all(arrays):
    any_spec = pl.BlockSpec(memory_space=pl.ANY)
    return pl.pallas_call(
        store_kernel,
        out_shape=tuple(jax.ShapeDtypeStruct(a.shape, a.dtype) for a in arrays),
        in_specs=[any_spec] * len(arrays),
        out_specs=(any_spec,) * len(arrays),
        scratch_shapes=[pltpu.SemaphoreType.DMA((len(arrays),))],
    )(*(pltpu.with_memory_space_constraint(a, pltpu.VMEM) for a in arrays))


def on_device(n, pas_q, pas_kv, pre_kv, d_out, passage_query, query_owner):
    count, tokens, width = pas_q.shape
    heads = width // HD
    part = pre_kv.shape[2]
    prefix = 2 * part
    assert pre_kv.shape[1] == 1
    block = (2, part, HD)
    any_spec = pl.BlockSpec(memory_space=pltpu.HBM)
    square = (count, heads, tokens, tokens)
    dma = pltpu.SemaphoreType.DMA
    call = pl.pallas_call(
        make_kernel(n, count, heads, tokens, part),
        out_shape=(
            jax.ShapeDtypeStruct(pas_q.shape, BF),
            jax.ShapeDtypeStruct(pas_q.shape, BF),
            jax.ShapeDtypeStruct(pas_kv.shape, BF),
            jax.ShapeDtypeStruct(pre_kv.shape, BF),
        ),
        in_specs=[any_spec] * 6,
        out_specs=(any_spec,) * 4,
        scratch_shapes=[
            pltpu.VMEM(pas_q.shape, BF),
            pltpu.VMEM(pas_q.shape, BF),
            pltpu.VMEM(pas_kv.shape, BF),
            pltpu.VMEM((count, heads, HD, tokens), BF),
            pltpu.VMEM((count, heads, HD, tokens), BF),
            pltpu.VMEM((2, count, HD, tokens), BF),
            pltpu.VMEM(square, F32),
            pltpu.VMEM(square, F32),
            pltpu.VMEM((count, heads, HD, tokens), F32),
            pltpu.VMEM((count, heads, prefix, tokens), BF),
            pltpu.VMEM((count, heads, HD, tokens), BF),
            pltpu.VMEM((count, heads, 8, tokens), F32),
            pltpu.VMEM((n, 2, 2, part, HD), BF),
            pltpu.VMEM((2, count, prefix, HD), BF),
            pltpu.VMEM((2, count, HD, prefix), BF),
            pltpu.VMEM((count, 2, prefix, HD), F32),
            pltpu.VMEM((count, 2, tokens, HD), F32),
            pltpu.VMEM(pas_q.shape, BF),
            pltpu.VMEM(pas_q.shape, BF),
            pltpu.VMEM(pas_kv.shape, BF),
            pltpu.VMEM(pre_kv.shape, BF),
            pltpu.VMEM((n,) + block, BF),
            pltpu.VMEM((n,) + block, BF),
            pltpu.VMEM((n,) + block, BF),
            pltpu.VMEM((n,) + block, BF),
            pltpu.SMEM(passage_query.shape, jnp.int32),
            pltpu.SMEM(query_owner.shape, jnp.int32),
            dma((5,)),
            dma((4,)),
            dma,
        ] + [dma((n,))] * 8,
        compiler_params=pltpu.CompilerParams(
            collective_id=0, has_side_effects=True, vmem_limit_bytes=40 * 1024 * 1024
        ),
    )
    arrays = (passage_query, query_owner, pas_q, pas_kv, pre_kv, d_out)
    return store_all(call(*(pltpu.with_memory_space_constraint(a, pltpu.HBM) for a in arrays)))


def solution(mesh):
    n = mesh.shape["dp"]

    def step(*arrays):
        return on_device(n, *arrays)

    return jax.shard_map(
        step,
        mesh=mesh,
        in_specs=(
            P(("groups", "dp", "seq"), None, "tensor"),
            P(None, ("groups", "dp", "seq"), None, "tensor"),
            P(None, ("groups", "dp"), "seq", "tensor"),
            P(("groups", "dp", "seq"), None, "tensor"),
            P("groups"),
            P("groups"),
        ),
        out_specs=(
            P(("groups", "dp", "seq"), None, "tensor"),
            P(("groups", "dp", "seq"), None, "tensor"),
            P(None, ("groups", "dp", "seq"), None, "tensor"),
            P(None, ("groups", "dp"), "seq", "tensor"),
        ),
        check_vma=False,
    )
```

```python
import math

import jax
import jax.numpy as jnp
from jax import lax
from jax.experimental import pallas as pl
from jax.experimental.pallas import tpu as pltpu
from jax.sharding import PartitionSpec as P

HD = 128
SCALE = HD ** (-0.5)
EXP_SCALE = SCALE * math.log2(math.e)
MASKED = -1e30
BF = jnp.bfloat16
F32 = jnp.float32
UNROLL = 4


def dot(a, b):
    return jnp.dot(a, b, preferred_element_type=F32)


def make_kernel(n, count, heads, tokens, part):
    prefix = 2 * part

    def kernel(
        pq_hbm, qo_hbm, q_hbm, kv_hbm, pre_hbm, do_hbm,
        out_hbm, dq_hbm, dkv_hbm, dpre_hbm,
        q, do, kv, q_t, do_t, kv_t, e_own, dp_own, o_own, ds_pre, o_t, stat,
        pre_k, pre_v, kv_pre, kv_pre_t, grad, own_grad, w_pre, out, dq, dkv, dpre,
        send1, recv1, send2, recv2,
        pq_ref, qo_ref, load_sem, store_sem, own_sem,
        zs_sem, zr_sem, fs_sem, fr_sem, s1_sem, r1_sem, s2_sem, r2_sem,
    ):
        z = lax.axis_index("dp")
        c = lax.axis_index("seq")
        other = 1 - c

        barrier = pltpu.get_barrier_semaphore()
        for d in range(1, n):
            pl.semaphore_signal(barrier, inc=1, device_id={"dp": lax.rem(z + d, n)})
        pl.semaphore_signal(barrier, inc=1, device_id={"seq": other})

        pre = (pre_k, pre_v)
        own = [
            pltpu.make_async_copy(pre_hbm.at[x, 0], pre[x].at[z, c], own_sem.at[x])
            for x in range(2)
        ]
        for copy in own:
            copy.start()
        loads = [
            pltpu.make_async_copy(q_hbm, q, load_sem.at[0]),
            pltpu.make_async_copy(kv_hbm, kv, load_sem.at[1]),
            pltpu.make_async_copy(do_hbm, do, load_sem.at[2]),
            pltpu.make_async_copy(pq_hbm, pq_ref, load_sem.at[3]),
            pltpu.make_async_copy(qo_hbm, qo_ref, load_sem.at[4]),
        ]
        for copy in loads:
            copy.start()

        for copy in own:
            copy.wait()
        pl.semaphore_wait(barrier, n)

        gathers = {}
        forwards = {}

        def send_stored(x):
            for d in range(1, n):
                gathers[x, d] = pltpu.make_async_remote_copy(
                    src_ref=pre[x].at[z, c], dst_ref=pre[x].at[z, c],
                    send_sem=zs_sem.at[x, d], recv_sem=zr_sem.at[x, d],
                    device_id={"dp": lax.rem(z + d, n)},
                )
                gathers[x, d].start()
            forwards[x, 0] = pltpu.make_async_remote_copy(
                src_ref=pre[x].at[z, c], dst_ref=pre[x].at[z, c],
                send_sem=fs_sem.at[x, 0], recv_sem=fr_sem.at[x, 0], device_id={"seq": other},
            )
            forwards[x, 0].start()

        def forward_arrived(x):
            for d in range(1, n):
                gathers[x, d].wait_recv()
                source = lax.rem(z + n - d, n)
                forwards[x, d] = pltpu.make_async_remote_copy(
                    src_ref=pre[x].at[source, c], dst_ref=pre[x].at[source, c],
                    send_sem=fs_sem.at[x, d], recv_sem=fr_sem.at[x, d],
                    device_id={"seq": other},
                )
                forwards[x, d].start()

        def pick_prefix(x):
            for d in range(n):
                forwards[x, d].wait_recv()
            for p in range(count):
                rows = pre[x][slots[p]].reshape(prefix, HD)
                kv_pre[x, p] = rows
                kv_pre_t[x, p] = rows.T

        pairs = {}
        spreads = {}

        def half_term(x, d, half):
            slot = lax.rem(z + d, n)
            rows = pl.ds(pl.multiple_of(half * part, part), part)
            value = None
            for p in range(count):
                use = jnp.where(slots[p] == slot, SCALE if x == 0 else 1.0, 0.0).astype(F32)
                term = grad[p, x, rows, :] * use
                value = term if value is None else value + term
            return value

        def send_pairs(x):
            for d in list(range(1, n)) + [0]:
                send1[x, d] = half_term(x, d, other).astype(BF)
                pairs[x, d] = pltpu.make_async_remote_copy(
                    src_ref=send1.at[x, d], dst_ref=recv1.at[x, d],
                    send_sem=s1_sem.at[x, d], recv_sem=r1_sem.at[x, d],
                    device_id={"seq": other},
                )
                pairs[x, d].start()

        def send_spreads(x):
            for d in range(1, n):
                value = half_term(x, d, c)
                pairs[x, d].wait_recv()
                send2[x, d] = (value + recv1[x, d].astype(F32)).astype(BF)
                spreads[x, d] = pltpu.make_async_remote_copy(
                    src_ref=send2.at[x, d], dst_ref=recv2.at[x, d],
                    send_sem=s2_sem.at[x, d], recv_sem=r2_sem.at[x, d],
                    device_id={"dp": lax.rem(z + d, n)},
                )
                spreads[x, d].start()

        def finish(x):
            total = half_term(x, 0, c)
            pairs[x, 0].wait_recv()
            total = total + recv1[x, 0].astype(F32)
            for d in range(1, n):
                spreads[x, d].wait_recv()
                total = total + recv2[x, d].astype(F32)
            dpre[x, 0] = total.astype(BF)

        send_stored(0)
        for copy in loads:
            copy.wait()
        first = (z * 2 + c) * count
        slots = [qo_ref[pq_ref[first + p]] for p in range(count)]

        for p in range(count):
            kv_t[0, p] = kv[0, p].T
            kv_t[1, p] = kv[1, p].T
        key_at = lax.broadcasted_iota(jnp.int32, (tokens, tokens), 0)
        token_at = lax.broadcasted_iota(jnp.int32, (tokens, tokens), 1)

        def over_heads(step):
            def body(h, carry):
                for p in range(count):
                    step(p, h, pl.ds(pl.multiple_of(h * HD, HD), HD))
                return carry

            lax.fori_loop(0, heads, body, 0, unroll=UNROLL)

        def own_scores(p, h, cols):
            qt = q[p, :, cols].T
            q_t[p, h] = qt
            scores = jnp.where(key_at <= token_at, dot(kv[0, p], qt), MASKED)
            top = jnp.max(scores, axis=0, keepdims=True)
            e = jnp.exp2((scores - top) * EXP_SCALE)
            stat[p, h, 0:1, :] = top
            stat[p, h, 1:2, :] = jnp.sum(e, axis=0, keepdims=True)
            e_own[p, h] = e

        def own_values(p, h, cols):
            dt = do[p, :, cols].T
            do_t[p, h] = dt
            o_own[p, h] = dot(kv_t[1, p], e_own[p, h].astype(BF))
            dp_own[p, h] = dot(kv[1, p], dt)

        def prefix_scores(p, h, cols):
            scores = dot(kv_pre[0, p], q_t[p, h])
            top_own = stat[p, h, 0:1, :]
            top = jnp.maximum(top_own, jnp.max(scores, axis=0, keepdims=True))
            shrink = jnp.exp2((top_own - top) * EXP_SCALE)
            e = jnp.exp2((scores - top) * EXP_SCALE)
            total = stat[p, h, 1:2, :] * shrink + jnp.sum(e, axis=0, keepdims=True)
            inverse = 1.0 / total
            w = e * inverse
            w_pre[p, h] = w
            stat[p, h, 2:3, :] = shrink * inverse
            grad[p, 1] += dot(w.astype(BF), do[p, :, cols])

        def own_value_grad(p, h, cols):
            w = e_own[p, h] * stat[p, h, 2:3, :]
            own_grad[p, 1] += dot(w.astype(BF), do[p, :, cols])

        def prefix_values(p, h, cols):
            dt = do_t[p, h]
            w = w_pre[p, h]
            o = o_own[p, h] * stat[p, h, 2:3, :] + dot(kv_pre_t[1, p], w.astype(BF))
            o = o.astype(BF)
            o_t[p, h] = o
            delta = jnp.sum(dt.astype(F32) * o.astype(F32), axis=0, keepdims=True)
            stat[p, h, 3:4, :] = delta
            ds = (w * (dot(kv_pre[1, p], dt) - delta)).astype(BF)
            ds_pre[p, h] = ds
            grad[p, 0] += dot(ds, q[p, :, cols])

        def own_rest(p, h, cols):
            w = e_own[p, h] * stat[p, h, 2:3, :]
            ds = (w * (dp_own[p, h] - stat[p, h, 3:4, :])).astype(BF)
            own_grad[p, 0] += dot(ds, q[p, :, cols])
            back = dot(kv_t[0, p], ds) + dot(kv_pre_t[0, p], ds_pre[p, h])
            dq[p, :, cols] = (back * SCALE).astype(BF).T

        grad[...] = jnp.zeros_like(grad)
        own_grad[...] = jnp.zeros_like(own_grad)
        send_stored(1)
        over_heads(own_scores)
        forward_arrived(0)
        over_heads(own_values)
        pick_prefix(0)
        over_heads(prefix_scores)
        send_pairs(1)
        forward_arrived(1)
        over_heads(own_value_grad)
        send_spreads(1)
        pick_prefix(1)
        over_heads(prefix_values)
        send_pairs(0)
        for p in range(count):
            for h in range(heads):
                out[p, :, h * HD:(h + 1) * HD] = o_t[p, h].T
        store_out = pltpu.make_async_copy(out, out_hbm, store_sem.at[0])
        store_out.start()
        send_spreads(0)
        over_heads(own_rest)
        store_dq = pltpu.make_async_copy(dq, dq_hbm, store_sem.at[1])
        store_dq.start()
        for p in range(count):
            dkv[0, p] = (own_grad[p, 0] * SCALE).astype(BF)
            dkv[1, p] = own_grad[p, 1].astype(BF)
        store_dkv = pltpu.make_async_copy(dkv, dkv_hbm, store_sem.at[2])
        store_dkv.start()
        finish(1)
        finish(0)
        store_dpre = pltpu.make_async_copy(dpre, dpre_hbm, store_sem.at[3])
        store_dpre.start()

        for x in range(2):
            for d in range(n):
                if d:
                    gathers[x, d].wait_send()
                    spreads[x, d].wait_send()
                forwards[x, d].wait_send()
                pairs[x, d].wait_send()
        store_out.wait()
        store_dq.wait()
        store_dkv.wait()
        store_dpre.wait()

    return kernel

def store_kernel(*refs):
    sems = refs[-1]
    count = (len(refs) - 1) // 2
    copies = [
        pltpu.make_async_copy(refs[i], refs[count + i], sems.at[i]) for i in range(count)
    ]
    for copy in copies:
        copy.start()
    for copy in copies:
        copy.wait()


def store_all(arrays):
    any_spec = pl.BlockSpec(memory_space=pl.ANY)
    return pl.pallas_call(
        store_kernel,
        out_shape=tuple(jax.ShapeDtypeStruct(a.shape, a.dtype) for a in arrays),
        in_specs=[any_spec] * len(arrays),
        out_specs=(any_spec,) * len(arrays),
        scratch_shapes=[pltpu.SemaphoreType.DMA((len(arrays),))],
    )(*(pltpu.with_memory_space_constraint(a, pltpu.VMEM) for a in arrays))


def on_device(n, pas_q, pas_kv, pre_kv, d_out, passage_query, query_owner):
    count, tokens, width = pas_q.shape
    heads = width // HD
    part = pre_kv.shape[2]
    prefix = 2 * part
    assert pre_kv.shape[1] == 1
    any_spec = pl.BlockSpec(memory_space=pltpu.HBM)
    square = (count, heads, tokens, tokens)
    dma = pltpu.SemaphoreType.DMA
    call = pl.pallas_call(
        make_kernel(n, count, heads, tokens, part),
        out_shape=(
            jax.ShapeDtypeStruct(pas_q.shape, BF),
            jax.ShapeDtypeStruct(pas_q.shape, BF),
            jax.ShapeDtypeStruct(pas_kv.shape, BF),
            jax.ShapeDtypeStruct(pre_kv.shape, BF),
        ),
        in_specs=[any_spec] * 6,
        out_specs=(any_spec,) * 4,
        scratch_shapes=[
            pltpu.VMEM(pas_q.shape, BF),
            pltpu.VMEM(pas_q.shape, BF),
            pltpu.VMEM(pas_kv.shape, BF),
            pltpu.VMEM((count, heads, HD, tokens), BF),
            pltpu.VMEM((count, heads, HD, tokens), BF),
            pltpu.VMEM((2, count, HD, tokens), BF),
            pltpu.VMEM(square, F32),
            pltpu.VMEM(square, F32),
            pltpu.VMEM((count, heads, HD, tokens), F32),
            pltpu.VMEM((count, heads, prefix, tokens), BF),
            pltpu.VMEM((count, heads, HD, tokens), BF),
            pltpu.VMEM((count, heads, 8, tokens), F32),
            pltpu.VMEM((n, 2, part, HD), BF),
            pltpu.VMEM((n, 2, part, HD), BF),
            pltpu.VMEM((2, count, prefix, HD), BF),
            pltpu.VMEM((2, count, HD, prefix), BF),
            pltpu.VMEM((count, 2, prefix, HD), F32),
            pltpu.VMEM((count, 2, tokens, HD), F32),
            pltpu.VMEM((count, heads, prefix, tokens), F32),
            pltpu.VMEM(pas_q.shape, BF),
            pltpu.VMEM(pas_q.shape, BF),
            pltpu.VMEM(pas_kv.shape, BF),
            pltpu.VMEM(pre_kv.shape, BF),
            pltpu.VMEM((2, n, part, HD), BF),
            pltpu.VMEM((2, n, part, HD), BF),
            pltpu.VMEM((2, n, part, HD), BF),
            pltpu.VMEM((2, n, part, HD), BF),
            pltpu.SMEM(passage_query.shape, jnp.int32),
            pltpu.SMEM(query_owner.shape, jnp.int32),
            dma((5,)),
            dma((4,)),
            dma((2,)),
        ] + [dma((2, n))] * 8,
        compiler_params=pltpu.CompilerParams(
            collective_id=0, has_side_effects=True, vmem_limit_bytes=40 * 1024 * 1024
        ),
    )
    arrays = (passage_query, query_owner, pas_q, pas_kv, pre_kv, d_out)
    return store_all(call(*(pltpu.with_memory_space_constraint(a, pltpu.HBM) for a in arrays)))


def solution(mesh):
    n = mesh.shape["dp"]

    def step(*arrays):
        return on_device(n, *arrays)

    return jax.shard_map(
        step,
        mesh=mesh,
        in_specs=(
            P(("groups", "dp", "seq"), None, "tensor"),
            P(None, ("groups", "dp", "seq"), None, "tensor"),
            P(None, ("groups", "dp"), "seq", "tensor"),
            P(("groups", "dp", "seq"), None, "tensor"),
            P("groups"),
            P("groups"),
        ),
        out_specs=(
            P(("groups", "dp", "seq"), None, "tensor"),
            P(("groups", "dp", "seq"), None, "tensor"),
            P(None, ("groups", "dp", "seq"), None, "tensor"),
            P(None, ("groups", "dp"), "seq", "tensor"),
        ),
        check_vma=False,
    )
```

```python
import math

import jax
import jax.numpy as jnp
from jax import lax
from jax.experimental import pallas as pl
from jax.experimental.pallas import tpu as pltpu
from jax.sharding import PartitionSpec as P

HD = 128
SCALE = HD ** (-0.5)
EXP_SCALE = SCALE * math.log2(math.e)
MASKED = -1e30
BF = jnp.bfloat16
F32 = jnp.float32


def dot(a, b):
    return jnp.dot(a, b, preferred_element_type=F32)


def make_kernel(n, count, heads, tokens, part):
    prefix = 2 * part
    order = list(range(1, n))

    def kernel(
        pq_hbm, qo_hbm, q_hbm, kv_hbm, pre_hbm, do_hbm,
        out, dq, dkv, dpre,
        q, do, kv, q_t, do_t, kv_t, e_own, dp_own, o_own, ds_pre, o_t, stat,
        pre_k, pre_v, kv_pre, kv_pre_t, grad, own_grad, total, w_pre,
        send1, recv1, send2, recv2,
        pq_ref, qo_ref, load_sem, own_sem,
        zs_sem, zr_sem, fs_sem, fr_sem, s1_sem, r1_sem, s2_sem, r2_sem,
    ):
        z = lax.axis_index("dp")
        c = lax.axis_index("seq")
        other = 1 - c

        barrier = pltpu.get_barrier_semaphore()
        for d in range(1, n):
            pl.semaphore_signal(barrier, inc=1, device_id={"dp": lax.rem(z + d, n)})
        pl.semaphore_signal(barrier, inc=1, device_id={"seq": other})

        pre = (pre_k, pre_v)
        own = [
            pltpu.make_async_copy(pre_hbm.at[x, 0], pre[x].at[z, c], own_sem.at[x])
            for x in range(2)
        ]
        for copy in own:
            copy.start()
        loads = [
            pltpu.make_async_copy(q_hbm, q, load_sem.at[0]),
            pltpu.make_async_copy(kv_hbm, kv, load_sem.at[1]),
            pltpu.make_async_copy(do_hbm, do, load_sem.at[2]),
            pltpu.make_async_copy(pq_hbm, pq_ref, load_sem.at[3]),
            pltpu.make_async_copy(qo_hbm, qo_ref, load_sem.at[4]),
        ]
        for copy in loads:
            copy.start()

        for copy in own:
            copy.wait()
        pl.semaphore_wait(barrier, n)

        gathers = {}
        forwards = {}

        def send_stored(x):
            for d in order:
                gathers[x, d] = pltpu.make_async_remote_copy(
                    src_ref=pre[x].at[z, c], dst_ref=pre[x].at[z, c],
                    send_sem=zs_sem.at[x, d], recv_sem=zr_sem.at[x, d],
                    device_id={"dp": lax.rem(z + d, n)},
                )
                gathers[x, d].start()
            forwards[x, 0] = pltpu.make_async_remote_copy(
                src_ref=pre[x].at[z, c], dst_ref=pre[x].at[z, c],
                send_sem=fs_sem.at[x, 0], recv_sem=fr_sem.at[x, 0], device_id={"seq": other},
            )
            forwards[x, 0].start()

        def forward_arrived(x):
            for d in order:
                gathers[x, d].wait_recv()
                source = lax.rem(z + n - d, n)
                forwards[x, d] = pltpu.make_async_remote_copy(
                    src_ref=pre[x].at[source, c], dst_ref=pre[x].at[source, c],
                    send_sem=fs_sem.at[x, d], recv_sem=fr_sem.at[x, d],
                    device_id={"seq": other},
                )
                forwards[x, d].start()

        def pick_prefix(x):
            for d in range(n):
                forwards[x, d].wait_recv()
            for p in range(count):
                rows = pre[x][slots[p]].reshape(prefix, HD)
                kv_pre[x, p] = rows
                kv_pre_t[x, p] = rows.T

        pairs = {}
        spreads = {}

        def half_term(x, d):
            slot = lax.rem(z + d, n)
            rows = pl.ds(pl.multiple_of(c * part, part), part)
            value = None
            for p in range(count):
                scale = SCALE if x == 0 else 1.0
                use = jnp.where(slots[p] == slot, scale, 0.0).astype(F32)
                use_far = jnp.where(far_slots[p] == slot, 1.0, 0.0).astype(F32)
                term = grad[p, x, rows, :] * use + recv1[x, p].astype(F32) * use_far
                value = term if value is None else value + term
            return value

        def send_pair(x, p):
            rows = pl.ds(pl.multiple_of(other * part, part), part)
            term = grad[p, x, rows, :]
            send1[x, p] = (term * SCALE if x == 0 else term).astype(BF)
            pairs[x, p] = pltpu.make_async_remote_copy(
                src_ref=send1.at[x, p], dst_ref=recv1.at[x, p],
                send_sem=s1_sem.at[x, p], recv_sem=r1_sem.at[x, p],
                device_id={"seq": other},
            )
            pairs[x, p].start()

        def send_spreads(x):
            for p in range(count):
                pairs[x, p].wait_recv()
            for d in order:
                send2[x, d] = half_term(x, d).astype(BF)
                spreads[x, d] = pltpu.make_async_remote_copy(
                    src_ref=send2.at[x, d], dst_ref=recv2.at[x, d],
                    send_sem=s2_sem.at[x, d], recv_sem=r2_sem.at[x, d],
                    device_id={"dp": lax.rem(z + d, n)},
                )
                spreads[x, d].start()
            total[x] = half_term(x, 0)

        def finish(x):
            value = total[x]
            for d in order:
                spreads[x, d].wait_recv()
                value = value + recv2[x, d].astype(F32)
            dpre[x, 0] = value.astype(BF)

        send_stored(0)
        for copy in loads:
            copy.wait()
        first = (z * 2 + c) * count
        slots = [qo_ref[pq_ref[first + p]] for p in range(count)]
        first_far = (z * 2 + other) * count
        far_slots = [qo_ref[pq_ref[first_far + p]] for p in range(count)]

        for p in range(count):
            kv_t[0, p] = kv[0, p].T
            kv_t[1, p] = kv[1, p].T
        key_at = lax.broadcasted_iota(jnp.int32, (tokens, tokens), 0)
        token_at = lax.broadcasted_iota(jnp.int32, (tokens, tokens), 1)

        def passage(step, p):
            for h in range(heads):
                step(p, h, slice(h * HD, (h + 1) * HD))

        def over_heads(step):
            for h in range(heads):
                for p in range(count):
                    step(p, h, slice(h * HD, (h + 1) * HD))

        def own_scores(p, h, cols):
            qt = q[p, :, cols].T
            q_t[p, h] = qt
            scores = jnp.where(key_at <= token_at, dot(kv[0, p], qt), MASKED)
            top = jnp.max(scores, axis=0, keepdims=True)
            e = jnp.exp2((scores - top) * EXP_SCALE)
            stat[p, h, 0:1, :] = top
            stat[p, h, 1:2, :] = jnp.sum(e, axis=0, keepdims=True)
            e_own[p, h] = e

        def own_values(p, h, cols):
            dt = do[p, :, cols].T
            do_t[p, h] = dt
            o_own[p, h] = dot(kv_t[1, p], e_own[p, h].astype(BF))
            dp_own[p, h] = dot(kv[1, p], dt)

        def prefix_scores(p, h, cols):
            scores = dot(kv_pre[0, p], q_t[p, h])
            top_own = stat[p, h, 0:1, :]
            top = jnp.maximum(top_own, jnp.max(scores, axis=0, keepdims=True))
            shrink = jnp.exp2((top_own - top) * EXP_SCALE)
            e = jnp.exp2((scores - top) * EXP_SCALE)
            norm = stat[p, h, 1:2, :] * shrink + jnp.sum(e, axis=0, keepdims=True)
            inverse = 1.0 / norm
            w = e * inverse
            w_pre[p, h] = w
            stat[p, h, 2:3, :] = shrink * inverse
            grad[p, 1] += dot(w.astype(BF), do[p, :, cols])

        def own_value_grad(p, h, cols):
            w = e_own[p, h] * stat[p, h, 2:3, :]
            own_grad[p, 1] += dot(w.astype(BF), do[p, :, cols])

        def prefix_values(p, h, cols):
            dt = do_t[p, h]
            w = w_pre[p, h]
            o = o_own[p, h] * stat[p, h, 2:3, :] + dot(kv_pre_t[1, p], w.astype(BF))
            o = o.astype(BF)
            o_t[p, h] = o
            delta = jnp.sum(dt.astype(F32) * o.astype(F32), axis=0, keepdims=True)
            stat[p, h, 3:4, :] = delta
            ds = (w * (dot(kv_pre[1, p], dt) - delta)).astype(BF)
            ds_pre[p, h] = ds
            grad[p, 0] += dot(ds, q[p, :, cols])

        def own_rest(p, h, cols):
            w = e_own[p, h] * stat[p, h, 2:3, :]
            ds = (w * (dp_own[p, h] - stat[p, h, 3:4, :])).astype(BF)
            own_grad[p, 0] += dot(ds, q[p, :, cols])
            back = dot(kv_t[0, p], ds) + dot(kv_pre_t[0, p], ds_pre[p, h])
            dq[p, :, cols] = (back * SCALE).astype(BF).T

        grad[...] = jnp.zeros_like(grad)
        own_grad[...] = jnp.zeros_like(own_grad)
        send_stored(1)
        over_heads(own_scores)
        forward_arrived(0)
        over_heads(own_values)
        pick_prefix(0)
        over_heads(prefix_scores)
        for p in range(count):
            send_pair(1, p)
        forward_arrived(1)
        over_heads(own_value_grad)
        send_spreads(1)
        pick_prefix(1)
        over_heads(prefix_values)
        for p in range(count):
            send_pair(0, p)
        for p in range(count):
            for h in range(heads):
                out[p, :, h * HD:(h + 1) * HD] = o_t[p, h].T
        send_spreads(0)
        over_heads(own_rest)
        for p in range(count):
            dkv[0, p] = (own_grad[p, 0] * SCALE).astype(BF)
            dkv[1, p] = own_grad[p, 1].astype(BF)
        finish(1)
        finish(0)

        for x in range(2):
            for d in range(n):
                if d:
                    gathers[x, d].wait_send()
                    spreads[x, d].wait_send()
                forwards[x, d].wait_send()
            for p in range(count):
                pairs[x, p].wait_send()

    return kernel

def store_kernel(*refs):
    sems = refs[-1]
    count = (len(refs) - 1) // 2
    copies = [
        pltpu.make_async_copy(refs[i], refs[count + i], sems.at[i]) for i in range(count)
    ]
    for copy in copies:
        copy.start()
    for copy in copies:
        copy.wait()


def store_all(arrays):
    any_spec = pl.BlockSpec(memory_space=pl.ANY)
    return pl.pallas_call(
        store_kernel,
        out_shape=tuple(jax.ShapeDtypeStruct(a.shape, a.dtype) for a in arrays),
        in_specs=[any_spec] * len(arrays),
        out_specs=(any_spec,) * len(arrays),
        scratch_shapes=[pltpu.SemaphoreType.DMA((len(arrays),))],
    )(*(pltpu.with_memory_space_constraint(a, pltpu.VMEM) for a in arrays))


def on_device(n, pas_q, pas_kv, pre_kv, d_out, passage_query, query_owner):
    count, tokens, width = pas_q.shape
    heads = width // HD
    part = pre_kv.shape[2]
    prefix = 2 * part
    assert pre_kv.shape[1] == 1
    any_spec = pl.BlockSpec(memory_space=pltpu.HBM)
    square = (count, heads, tokens, tokens)
    dma = pltpu.SemaphoreType.DMA
    call = pl.pallas_call(
        make_kernel(n, count, heads, tokens, part),
        out_shape=(
            jax.ShapeDtypeStruct(pas_q.shape, BF),
            jax.ShapeDtypeStruct(pas_q.shape, BF),
            jax.ShapeDtypeStruct(pas_kv.shape, BF),
            jax.ShapeDtypeStruct(pre_kv.shape, BF),
        ),
        in_specs=[any_spec] * 6,
        out_specs=(pl.BlockSpec(memory_space=pltpu.VMEM),) * 4,
        scratch_shapes=[
            pltpu.VMEM(pas_q.shape, BF),
            pltpu.VMEM(pas_q.shape, BF),
            pltpu.VMEM(pas_kv.shape, BF),
            pltpu.VMEM((count, heads, HD, tokens), BF),
            pltpu.VMEM((count, heads, HD, tokens), BF),
            pltpu.VMEM((2, count, HD, tokens), BF),
            pltpu.VMEM(square, F32),
            pltpu.VMEM(square, F32),
            pltpu.VMEM((count, heads, HD, tokens), F32),
            pltpu.VMEM((count, heads, prefix, tokens), BF),
            pltpu.VMEM((count, heads, HD, tokens), BF),
            pltpu.VMEM((count, heads, 8, tokens), F32),
            pltpu.VMEM((n, 2, part, HD), BF),
            pltpu.VMEM((n, 2, part, HD), BF),
            pltpu.VMEM((2, count, prefix, HD), BF),
            pltpu.VMEM((2, count, HD, prefix), BF),
            pltpu.VMEM((count, 2, prefix, HD), F32),
            pltpu.VMEM((count, 2, tokens, HD), F32),
            pltpu.VMEM((2, part, HD), F32),
            pltpu.VMEM((count, heads, prefix, tokens), F32),
            pltpu.VMEM((2, count, part, HD), BF),
            pltpu.VMEM((2, count, part, HD), BF),
            pltpu.VMEM((2, n, part, HD), BF),
            pltpu.VMEM((2, n, part, HD), BF),
            pltpu.SMEM(passage_query.shape, jnp.int32),
            pltpu.SMEM(query_owner.shape, jnp.int32),
            dma((5,)),
            dma((2,)),
        ] + [dma((2, n))] * 4 + [dma((2, count))] * 2 + [dma((2, n))] * 2,
        compiler_params=pltpu.CompilerParams(
            collective_id=0, has_side_effects=True, vmem_limit_bytes=40 * 1024 * 1024
        ),
    )
    arrays = (passage_query, query_owner, pas_q, pas_kv, pre_kv, d_out)
    return store_all(call(*(pltpu.with_memory_space_constraint(a, pltpu.HBM) for a in arrays)))


def solution(mesh):
    n = mesh.shape["dp"]

    def step(*arrays):
        return on_device(n, *arrays)

    return jax.shard_map(
        step,
        mesh=mesh,
        in_specs=(
            P(("groups", "dp", "seq"), None, "tensor"),
            P(None, ("groups", "dp", "seq"), None, "tensor"),
            P(None, ("groups", "dp"), "seq", "tensor"),
            P(("groups", "dp", "seq"), None, "tensor"),
            P("groups"),
            P("groups"),
        ),
        out_specs=(
            P(("groups", "dp", "seq"), None, "tensor"),
            P(("groups", "dp", "seq"), None, "tensor"),
            P(None, ("groups", "dp", "seq"), None, "tensor"),
            P(None, ("groups", "dp"), "seq", "tensor"),
        ),
        check_vma=False,
    )
```

```python
import math

import jax
import jax.numpy as jnp
from jax import lax
from jax.experimental import pallas as pl
from jax.experimental.pallas import tpu as pltpu
from jax.sharding import PartitionSpec as P

HD = 128
SCALE = HD ** (-0.5)
EXP_SCALE = SCALE * math.log2(math.e)
MASKED = -1e30
BF = jnp.bfloat16
F32 = jnp.float32


def dot(a, b):
    return jnp.dot(a, b, preferred_element_type=F32)


def make_kernel(n, count, heads, tokens, part):
    prefix = 2 * part
    order = list(range(1, n))

    def kernel(
        pq_hbm, qo_hbm, q_hbm, kv_hbm, pre_hbm, do_hbm,
        out, dq, dkv, dpre,
        q, do, kv, q_t, do_t, kv_t, e_own, dp_own, o_own, ds_pre, o_t, stat,
        pre_k, pre_v, kv_pre, kv_pre_t, grad, own_grad, total, near, w_pre,
        send1, recv1, send2, recv2,
        pq_ref, qo_ref, load_sem, own_sem,
        zs_sem, zr_sem, fs_sem, fr_sem, s1_sem, r1_sem, s2_sem, r2_sem,
    ):
        z = lax.axis_index("dp")
        c = lax.axis_index("seq")
        other = 1 - c

        barrier = pltpu.get_barrier_semaphore()
        for d in range(1, n):
            pl.semaphore_signal(barrier, inc=1, device_id={"dp": lax.rem(z + d, n)})
        pl.semaphore_signal(barrier, inc=1, device_id={"seq": other})

        pre = (pre_k, pre_v)
        own = [
            pltpu.make_async_copy(pre_hbm.at[x, 0], pre[x].at[z, c], own_sem.at[x])
            for x in range(2)
        ]
        for copy in own:
            copy.start()
        loads = [
            pltpu.make_async_copy(q_hbm, q, load_sem.at[0]),
            pltpu.make_async_copy(kv_hbm, kv, load_sem.at[1]),
            pltpu.make_async_copy(do_hbm, do, load_sem.at[2]),
            pltpu.make_async_copy(pq_hbm, pq_ref, load_sem.at[3]),
            pltpu.make_async_copy(qo_hbm, qo_ref, load_sem.at[4]),
        ]
        for copy in loads:
            copy.start()

        for copy in own:
            copy.wait()
        pl.semaphore_wait(barrier, n)

        gathers = {}
        forwards = {}

        def send_stored(x):
            for d in order:
                gathers[x, d] = pltpu.make_async_remote_copy(
                    src_ref=pre[x].at[z, c], dst_ref=pre[x].at[z, c],
                    send_sem=zs_sem.at[x, d], recv_sem=zr_sem.at[x, d],
                    device_id={"dp": lax.rem(z + d, n)},
                )
                gathers[x, d].start()
            forwards[x, 0] = pltpu.make_async_remote_copy(
                src_ref=pre[x].at[z, c], dst_ref=pre[x].at[z, c],
                send_sem=fs_sem.at[x, 0], recv_sem=fr_sem.at[x, 0], device_id={"seq": other},
            )
            forwards[x, 0].start()

        def forward_arrived(x):
            for d in order:
                gathers[x, d].wait_recv()
                source = lax.rem(z + n - d, n)
                forwards[x, d] = pltpu.make_async_remote_copy(
                    src_ref=pre[x].at[source, c], dst_ref=pre[x].at[source, c],
                    send_sem=fs_sem.at[x, d], recv_sem=fr_sem.at[x, d],
                    device_id={"seq": other},
                )
                forwards[x, d].start()

        def pick_prefix(x):
            for d in range(n):
                forwards[x, d].wait_recv()
            for p in range(count):
                rows = pre[x][slots[p]].reshape(prefix, HD)
                kv_pre[x, p] = rows
                kv_pre_t[x, p] = rows.T

        pairs = {}
        spreads = {}

        def use(at, p, d):
            return jnp.where(at[p] == lax.rem(z + d, n), 1.0, 0.0).astype(F32)

        def near_term(x, d):
            rows = pl.ds(pl.multiple_of(c * part, part), part)
            scale = SCALE if x == 0 else 1.0
            return sum(grad[p, x, rows, :] * (use(slots, p, d) * scale) for p in range(count))

        def far_term(x, d):
            return sum(recv1[x, p].astype(F32) * use(far_slots, p, d) for p in range(count))

        def send_pair(x, p):
            rows = pl.ds(pl.multiple_of(other * part, part), part)
            term = grad[p, x, rows, :]
            send1[x, p] = (term * SCALE if x == 0 else term).astype(BF)
            pairs[x, p] = pltpu.make_async_remote_copy(
                src_ref=send1.at[x, p], dst_ref=recv1.at[x, p],
                send_sem=s1_sem.at[x, p], recv_sem=r1_sem.at[x, p],
                device_id={"seq": other},
            )
            pairs[x, p].start()

        def send_spreads(x):
            for d in range(n):
                near[d] = near_term(x, d)
            for p in range(count):
                pairs[x, p].wait_recv()
            for d in order:
                send2[x, d] = (near[d] + far_term(x, d)).astype(BF)
                spreads[x, d] = pltpu.make_async_remote_copy(
                    src_ref=send2.at[x, d], dst_ref=recv2.at[x, d],
                    send_sem=s2_sem.at[x, d], recv_sem=r2_sem.at[x, d],
                    device_id={"dp": lax.rem(z + d, n)},
                )
                spreads[x, d].start()
            total[x] = near[0] + far_term(x, 0)

        def finish(x):
            value = total[x]
            for d in order:
                spreads[x, d].wait_recv()
                value = value + recv2[x, d].astype(F32)
            dpre[x, 0] = value.astype(BF)

        send_stored(0)
        for copy in loads:
            copy.wait()
        first = (z * 2 + c) * count
        slots = [qo_ref[pq_ref[first + p]] for p in range(count)]
        first_far = (z * 2 + other) * count
        far_slots = [qo_ref[pq_ref[first_far + p]] for p in range(count)]

        for p in range(count):
            kv_t[0, p] = kv[0, p].T
            kv_t[1, p] = kv[1, p].T
        key_at = lax.broadcasted_iota(jnp.int32, (tokens, tokens), 0)
        token_at = lax.broadcasted_iota(jnp.int32, (tokens, tokens), 1)

        def passage(step, p):
            for h in range(heads):
                step(p, h, slice(h * HD, (h + 1) * HD))

        def over_heads(step):
            for h in range(heads):
                for p in range(count):
                    step(p, h, slice(h * HD, (h + 1) * HD))

        def own_scores(p, h, cols):
            qt = q[p, :, cols].T
            q_t[p, h] = qt
            scores = jnp.where(key_at <= token_at, dot(kv[0, p], qt), MASKED)
            top = jnp.max(scores, axis=0, keepdims=True)
            e = jnp.exp2((scores - top) * EXP_SCALE)
            stat[p, h, 0:1, :] = top
            stat[p, h, 1:2, :] = jnp.sum(e, axis=0, keepdims=True)
            e_own[p, h] = e

        def own_values(p, h, cols):
            dt = do[p, :, cols].T
            do_t[p, h] = dt
            o_own[p, h] = dot(kv_t[1, p], e_own[p, h].astype(BF))
            dp_own[p, h] = dot(kv[1, p], dt)

        def prefix_scores(p, h, cols):
            scores = dot(kv_pre[0, p], q_t[p, h])
            top_own = stat[p, h, 0:1, :]
            top = jnp.maximum(top_own, jnp.max(scores, axis=0, keepdims=True))
            shrink = jnp.exp2((top_own - top) * EXP_SCALE)
            e = jnp.exp2((scores - top) * EXP_SCALE)
            norm = stat[p, h, 1:2, :] * shrink + jnp.sum(e, axis=0, keepdims=True)
            inverse = 1.0 / norm
            w = e * inverse
            w_pre[p, h] = w
            stat[p, h, 2:3, :] = shrink * inverse
            grad[p, 1] += dot(w.astype(BF), do[p, :, cols])

        def own_value_grad(p, h, cols):
            w = e_own[p, h] * stat[p, h, 2:3, :]
            own_grad[p, 1] += dot(w.astype(BF), do[p, :, cols])

        def prefix_values(p, h, cols):
            dt = do_t[p, h]
            w = w_pre[p, h]
            o = o_own[p, h] * stat[p, h, 2:3, :] + dot(kv_pre_t[1, p], w.astype(BF))
            o = o.astype(BF)
            o_t[p, h] = o
            delta = jnp.sum(dt.astype(F32) * o.astype(F32), axis=0, keepdims=True)
            stat[p, h, 3:4, :] = delta
            ds = (w * (dot(kv_pre[1, p], dt) - delta)).astype(BF)
            ds_pre[p, h] = ds
            grad[p, 0] += dot(ds, q[p, :, cols])

        def own_rest(p, h, cols):
            w = e_own[p, h] * stat[p, h, 2:3, :]
            ds = (w * (dp_own[p, h] - stat[p, h, 3:4, :])).astype(BF)
            own_grad[p, 0] += dot(ds, q[p, :, cols])
            back = dot(kv_t[0, p], ds) + dot(kv_pre_t[0, p], ds_pre[p, h])
            dq[p, :, cols] = (back * SCALE).astype(BF).T

        grad[...] = jnp.zeros_like(grad)
        own_grad[...] = jnp.zeros_like(own_grad)
        send_stored(1)
        over_heads(own_scores)
        forward_arrived(0)
        over_heads(own_values)
        pick_prefix(0)
        over_heads(prefix_scores)
        for p in range(count):
            send_pair(1, p)
        forward_arrived(1)
        over_heads(own_value_grad)
        send_spreads(1)
        pick_prefix(1)
        over_heads(prefix_values)
        for p in range(count):
            send_pair(0, p)
        for p in range(count):
            for h in range(heads):
                out[p, :, h * HD:(h + 1) * HD] = o_t[p, h].T
        send_spreads(0)
        over_heads(own_rest)
        for p in range(count):
            dkv[0, p] = (own_grad[p, 0] * SCALE).astype(BF)
            dkv[1, p] = own_grad[p, 1].astype(BF)
        finish(1)
        finish(0)

        for x in range(2):
            for d in range(n):
                if d:
                    gathers[x, d].wait_send()
                    spreads[x, d].wait_send()
                forwards[x, d].wait_send()
            for p in range(count):
                pairs[x, p].wait_send()

    return kernel

def store_kernel(*refs):
    sems = refs[-1]
    count = (len(refs) - 1) // 2
    copies = [
        pltpu.make_async_copy(refs[i], refs[count + i], sems.at[i]) for i in range(count)
    ]
    for copy in copies:
        copy.start()
    for copy in copies:
        copy.wait()


def store_all(arrays):
    any_spec = pl.BlockSpec(memory_space=pl.ANY)
    return pl.pallas_call(
        store_kernel,
        out_shape=tuple(jax.ShapeDtypeStruct(a.shape, a.dtype) for a in arrays),
        in_specs=[any_spec] * len(arrays),
        out_specs=(any_spec,) * len(arrays),
        scratch_shapes=[pltpu.SemaphoreType.DMA((len(arrays),))],
    )(*(pltpu.with_memory_space_constraint(a, pltpu.VMEM) for a in arrays))


def on_device(n, pas_q, pas_kv, pre_kv, d_out, passage_query, query_owner):
    count, tokens, width = pas_q.shape
    heads = width // HD
    part = pre_kv.shape[2]
    prefix = 2 * part
    assert pre_kv.shape[1] == 1
    any_spec = pl.BlockSpec(memory_space=pltpu.HBM)
    square = (count, heads, tokens, tokens)
    dma = pltpu.SemaphoreType.DMA
    call = pl.pallas_call(
        make_kernel(n, count, heads, tokens, part),
        out_shape=(
            jax.ShapeDtypeStruct(pas_q.shape, BF),
            jax.ShapeDtypeStruct(pas_q.shape, BF),
            jax.ShapeDtypeStruct(pas_kv.shape, BF),
            jax.ShapeDtypeStruct(pre_kv.shape, BF),
        ),
        in_specs=[any_spec] * 6,
        out_specs=(pl.BlockSpec(memory_space=pltpu.VMEM),) * 4,
        scratch_shapes=[
            pltpu.VMEM(pas_q.shape, BF),
            pltpu.VMEM(pas_q.shape, BF),
            pltpu.VMEM(pas_kv.shape, BF),
            pltpu.VMEM((count, heads, HD, tokens), BF),
            pltpu.VMEM((count, heads, HD, tokens), BF),
            pltpu.VMEM((2, count, HD, tokens), BF),
            pltpu.VMEM(square, F32),
            pltpu.VMEM(square, F32),
            pltpu.VMEM((count, heads, HD, tokens), F32),
            pltpu.VMEM((count, heads, prefix, tokens), BF),
            pltpu.VMEM((count, heads, HD, tokens), BF),
            pltpu.VMEM((count, heads, 8, tokens), F32),
            pltpu.VMEM((n, 2, part, HD), BF),
            pltpu.VMEM((n, 2, part, HD), BF),
            pltpu.VMEM((2, count, prefix, HD), BF),
            pltpu.VMEM((2, count, HD, prefix), BF),
            pltpu.VMEM((count, 2, prefix, HD), F32),
            pltpu.VMEM((count, 2, tokens, HD), F32),
            pltpu.VMEM((2, part, HD), F32),
            pltpu.VMEM((n, part, HD), F32),
            pltpu.VMEM((count, heads, prefix, tokens), F32),
            pltpu.VMEM((2, count, part, HD), BF),
            pltpu.VMEM((2, count, part, HD), BF),
            pltpu.VMEM((2, n, part, HD), BF),
            pltpu.VMEM((2, n, part, HD), BF),
            pltpu.SMEM(passage_query.shape, jnp.int32),
            pltpu.SMEM(query_owner.shape, jnp.int32),
            dma((5,)),
            dma((2,)),
        ] + [dma((2, n))] * 4 + [dma((2, count))] * 2 + [dma((2, n))] * 2,
        compiler_params=pltpu.CompilerParams(
            collective_id=0, has_side_effects=True, vmem_limit_bytes=40 * 1024 * 1024
        ),
    )
    arrays = (passage_query, query_owner, pas_q, pas_kv, pre_kv, d_out)
    return store_all(call(*(pltpu.with_memory_space_constraint(a, pltpu.HBM) for a in arrays)))


def solution(mesh):
    n = mesh.shape["dp"]

    def step(*arrays):
        return on_device(n, *arrays)

    return jax.shard_map(
        step,
        mesh=mesh,
        in_specs=(
            P(("groups", "dp", "seq"), None, "tensor"),
            P(None, ("groups", "dp", "seq"), None, "tensor"),
            P(None, ("groups", "dp"), "seq", "tensor"),
            P(("groups", "dp", "seq"), None, "tensor"),
            P("groups"),
            P("groups"),
        ),
        out_specs=(
            P(("groups", "dp", "seq"), None, "tensor"),
            P(("groups", "dp", "seq"), None, "tensor"),
            P(None, ("groups", "dp", "seq"), None, "tensor"),
            P(None, ("groups", "dp"), "seq", "tensor"),
        ),
        check_vma=False,
    )
```
